32 devices in a mesh: dp: 4 (over y, x), row: 2 (over core), col: 4 (over z).
Axes of the slice: x: 2, y: 2, z: 4, core: 2. Of those that a mesh axis runs over, the one named last changes fastest.
Arguments:
- step_count: int32 [1], replicated, may hold values from 2 to 11
- ffn_weight: bfloat16 [4096, 10240], P('row', 'col'), may hold values from -40 to 40
- ffn_grads: float32 [4, 4096, 10240], P('dp', 'row', 'col'), may hold values from -80 to 80
- ffn_rows: float32 [4096], P('row'), may hold values from 0.1 to 12
- ffn_cols: float32 [10240], P('col'), may hold values from 0.1 to 1
- attn_weight: bfloat16 [4096, 4096], P('row', 'col'), may hold values from -40 to 40
- attn_grads: float32 [4, 4096, 4096], P('dp', 'row', 'col'), may hold values from -80 to 80
- attn_rows: float32 [4096], P('row'), may hold values from 0.1 to 12
- attn_cols: float32 [4096], P('col'), may hold values from 0.1 to 1
Outputs:
- ffn_weight_new: float32 [4096, 10240], P('row', 'col')
- ffn_update: float32 [4096, 10240], P('row', 'col')
- ffn_rows_new: float32 [4096], P('row')
- ffn_cols_new: float32 [10240], P('col')
- attn_weight_new: float32 [4096, 4096], P('row', 'col')
- attn_update: float32 [4096, 4096], P('row', 'col')
- attn_rows_new: float32 [4096], P('row')
- attn_cols_new: float32 [4096], P('col')
The draws below stay inside these ranges and needn't reach their ends.
All inputs are finite; a program needn't handle non-finite values.
Results may differ from the reference program's by a relative error of at most 0.0003.
Values sent between devices are 32-bit elements; how exact they have to be, the bound alone decides.
A program may use at most 320 MiB of HBM per device.

```python
import math
import jax
import jax.numpy as jnp
from jax import lax

D = 4096
FF = 10240
INNER = 4096
N_DP = 4


def rising(count):
    spread = 6.0
    place = jnp.arange(count).astype(jnp.float32) / (count - 1)
    return jnp.exp(math.log(spread) * place)


def weight_draw(key, width):
    rough = jax.random.uniform(jax.random.fold_in(key, 3), (D, width), jnp.float32, 0.6, 1.4)
    base = jax.random.truncated_normal(jax.random.fold_in(key, 4), -4.0, 4.0, (D, width), jnp.float32)
    return (0.4 * rising(D)[:, None] * rough * base).astype(jnp.bfloat16)


def grad_draw(key, width):
    scale = 0.05
    base = jax.random.truncated_normal(jax.random.fold_in(key, 5), -6.0, 6.0, (N_DP, D, width), jnp.float32)
    rough = jax.random.uniform(jax.random.fold_in(key, 6), (N_DP, D, width), jnp.float32, 0.6, 1.4)
    return scale * rising(D)[None, :, None] * rough * base


def moment_draw(key):
    level = jax.random.uniform(jax.random.fold_in(key, 7), (D,), jnp.float32, math.log(0.1), 0.0)
    return jnp.exp(level) * rising(D)


def draw_ffn_weight(key, part):
    key = jax.random.fold_in(key, 11)
    return weight_draw(key, FF)


def draw_attn_weight(key, part):
    key = jax.random.fold_in(key, 12)
    return weight_draw(key, INNER)


def draw_ffn_grads(key, part):
    key = jax.random.fold_in(key, 13)
    return grad_draw(key, FF)


def draw_attn_grads(key, part):
    key = jax.random.fold_in(key, 14)
    return grad_draw(key, INNER)


def draw_ffn_rows(key, part):
    key = jax.random.fold_in(key, 15)
    return moment_draw(key)


def draw_attn_rows(key, part):
    key = jax.random.fold_in(key, 16)
    return moment_draw(key)


def shard_levels(key, shape, cuts, least, largest):
    def one(axis_at, shards_of):
        steps = jax.random.uniform(jax.random.fold_in(jax.random.fold_in(key, 6), axis_at), (shards_of,), jnp.float32, least / len(cuts), largest / len(cuts))
        return jnp.repeat(jnp.exp(steps), shape[axis_at] // shards_of).reshape((-1,) + (1,) * (len(shape) - axis_at - 1))

    level = one(*cuts[0])
    for cut in cuts[1:]:
        level = level * one(*cut)
    return level


def setup_inputs(seed: int = 0) -> dict:
    streams_of = jax.random.split(jax.random.key(seed), 10)
    step_count = jax.random.randint(streams_of[0], (1,), 2, 12).astype(jnp.int32)
    ffn_weight = draw_ffn_weight(jax.random.fold_in(streams_of[9], 71), 0)
    ffn_grads = draw_ffn_grads(jax.random.fold_in(streams_of[9], 71), 0)
    ffn_rows = draw_ffn_rows(jax.random.fold_in(streams_of[9], 71), 0)
    ffn_cols = jnp.clip(jnp.exp(math.log(1.0) - 2.3025851 * jax.random.uniform(streams_of[4], (FF,), jnp.float32) ** shard_levels(streams_of[4], (FF,), ((0, 4),), -0.2, 0.2)), 0.1, 1.0)
    attn_weight = draw_attn_weight(jax.random.fold_in(streams_of[9], 71), 0)
    attn_grads = draw_attn_grads(jax.random.fold_in(streams_of[9], 71), 0)
    attn_rows = draw_attn_rows(jax.random.fold_in(streams_of[9], 71), 0)
    attn_cols = jnp.clip(jnp.exp(math.log(1.0) - 2.3025851 * jax.random.uniform(streams_of[8], (INNER,), jnp.float32) ** shard_levels(streams_of[8], (INNER,), ((0, 4),), -0.2, 0.2)), 0.1, 1.0)
    return dict(step_count=step_count, ffn_weight=ffn_weight, ffn_grads=ffn_grads, ffn_rows=ffn_rows, ffn_cols=ffn_cols, attn_weight=attn_weight, attn_grads=attn_grads, attn_rows=attn_rows, attn_cols=attn_cols)


def adafactor(weight, grads, rows_old, cols_old, decay):
    summed = lax.optimization_barrier(jnp.sum(grads, axis=0))
    squares = summed * summed + 1e-30
    rows_new = decay * rows_old + (1.0 - decay) * lax.optimization_barrier(jnp.mean(squares, axis=1))
    cols_new = decay * cols_old + (1.0 - decay) * lax.optimization_barrier(jnp.mean(squares, axis=0))
    second = rows_new[:, None] * cols_new[None, :] / jnp.mean(rows_new)
    raw_update = summed / jnp.sqrt(second)
    update_rms = jnp.sqrt(jnp.mean(raw_update * raw_update))
    update = raw_update / jnp.maximum(1.0, update_rms)
    wide = weight.astype(jnp.float32)
    weight_rms = jnp.sqrt(jnp.mean(wide * wide))
    weight_new = wide - 0.01 * weight_rms * update
    return (weight_new, update, rows_new, cols_new)

def reference(step_count, ffn_weight, ffn_grads, ffn_rows, ffn_cols, attn_weight, attn_grads, attn_rows, attn_cols):
    step_value = step_count[0].astype(jnp.float32)
    decay = 1.0 - step_value ** (-0.8)
    first = adafactor(ffn_weight, ffn_grads, ffn_rows, ffn_cols, decay)
    second = adafactor(attn_weight, attn_grads, attn_rows, attn_cols, decay)
    return (first[0], first[1], first[2], first[3], second[0], second[1], second[2], second[3])
```

```python
import jax
import jax.numpy as jnp
from jax import lax
from jax.sharding import PartitionSpec as P


def apply_step(w_tile, factor, update):
    return w_tile.astype(jnp.float32) - factor * update


def body(
    step_count,
    ffn_weight,
    ffn_grads,
    ffn_rows,
    ffn_cols,
    attn_weight,
    attn_grads,
    attn_rows,
    attn_cols,
):
    step_value = step_count[0].astype(jnp.float32)
    decay = 1.0 - step_value ** (-0.8)
    weights = (ffn_weight, attn_weight)
    rows_old = (ffn_rows, attn_rows)
    cols_old = (ffn_cols, attn_cols)
    row_devs = lax.axis_size("row")
    col_devs = lax.axis_size("col")
    widths_in = tuple((w_tile.shape[0] * row_devs for w_tile in weights))
    widths_out = tuple((w_tile.shape[1] * col_devs for w_tile in weights))
    summed = (
        lax.psum_scatter(ffn_grads[0], "dp", scatter_dimension=0, tiled=True),
        lax.psum_scatter(attn_grads[0], "dp", scatter_dimension=0, tiled=True),
    )
    whole = tuple(lax.all_gather(g_part, "dp", axis=0, tiled=True) for g_part in summed)
    share_rows = summed[0].shape[0]
    offset = lax.axis_index("dp") * share_rows
    squares = tuple((g_part * g_part + 1e-30 for g_part in summed))
    row_sums = lax.psum(tuple((jnp.sum(s_part, axis=1) for s_part in squares)), "col")
    col_part = tuple((jnp.sum(s_part, axis=0) for s_part in squares))
    row_full = lax.all_gather(row_sums, "dp", axis=0, tiled=True)
    col_sums = lax.psum(col_part, ("dp", "row"))
    rows_new = tuple(
        (
            decay * rows_old[index] + (1.0 - decay) * (row_full[index] / widths_out[index])
            for index in range(2)
        )
    )
    cols_new = tuple(
        (
            decay * cols_old[index] + (1.0 - decay) * (col_sums[index] / widths_in[index])
            for index in range(2)
        )
    )
    masses = lax.psum(tuple((jnp.sum(r_tile) for r_tile in rows_new)), "row")
    raw_updates = []
    update_sq = []
    for index in range(2):
        row_own = lax.dynamic_slice_in_dim(rows_new[index], offset, share_rows, 0)
        second = row_own[:, None] * cols_new[index][None, :] / (masses[index] / widths_in[index])
        raw_update = summed[index] / jnp.sqrt(second)
        raw_updates.append(raw_update)
        update_sq.append(jnp.sum(raw_update * raw_update))
    update_tot = lax.psum((update_sq[0], update_sq[1]), ("dp", "row", "col"))
    weight_tot = lax.psum(
        tuple((jnp.sum(jnp.square(w_tile.astype(jnp.float32))) for w_tile in weights)),
        ("row", "col"),
    )
    totals = tuple(update_tot) + tuple(weight_tot)
    clipped = []
    fresh = []
    for index in range(2):
        entries = widths_in[index] * widths_out[index]
        update_rms = jnp.sqrt(totals[index] / entries)
        factor = 0.01 * jnp.sqrt(totals[2 + index] / entries)
        mean = masses[index] / widths_in[index]
        second = rows_new[index][:, None] * cols_new[index][None, :] / mean
        update = whole[index] / jnp.sqrt(second) / jnp.maximum(1.0, update_rms)
        clipped.append(update)
        fresh.append(apply_step(weights[index], factor, update))
    return (
        fresh[0],
        clipped[0],
        rows_new[0],
        cols_new[0],
        fresh[1],
        clipped[1],
        rows_new[1],
        cols_new[1],
    )


def solution(mesh):
    in_specs = (
        P(),
        P("row", "col"),
        P("dp", "row", "col"),
        P("row"),
        P("col"),
        P("row", "col"),
        P("dp", "row", "col"),
        P("row"),
        P("col"),
    )
    out_specs = (
        P("row", "col"),
        P("row", "col"),
        P("row"),
        P("col"),
        P("row", "col"),
        P("row", "col"),
        P("row"),
        P("col"),
    )
    return jax.shard_map(body, mesh=mesh, in_specs=in_specs, out_specs=out_specs, check_vma=False)
```

```python
import functools

import jax
import jax.numpy as jnp
from jax import lax
from jax.experimental import pallas as pl
from jax.experimental.pallas import tpu as pltpu
from jax.sharding import PartitionSpec as P

MESH = pl.DeviceIdType.MESH
LANES = 128
STRIP = 8
CUTS = (4, 2)


def gray(index):
    high = index // 2
    return index + high * (5 - 2 * index)


def lane_sums(x):
    total = x[:, :LANES]
    for c in range(1, x.shape[1] // LANES):
        total = total + x[:, c * LANES : (c + 1) * LANES]
    return total


def to_lanes(ref, out_ref, at):
    rows = ref.shape[0]
    for c in range(rows // LANES):
        turned = ref[pl.ds(c * LANES, LANES), :].T
        out_ref[:, pl.ds(at + c * LANES, LANES)] = jnp.sum(turned, axis=0, keepdims=True)


def kernel(
    sizes,
    decay_ref,
    g1, g2, w1, w2, r1, r2, c1, c2,
    full1, full2, rn1, rn2, cn1, cn2, tot,
    rb1, rb2, lb1, lb2, wb1, wb2, ca1, ca2, rp1, rp2, ic1, ic2,
    row_msg, col_msg, upd_msg, end_msg,
    own_row, own_col, own_upd, own_end,
    send_sem, recv_sem, load_sem, keep_sem, w_sem,
    s_row, q_row, s_col, q_col, s_upd, q_upd, s_end, q_end,
):
    dp_n, row_n, col_n = sizes
    grads, fulls, rbs, lbs = (g1, g2), (full1, full2), (rb1, rb2), (lb1, lb2)
    wts, wbs, cas, rps, ics = (w1, w2), (wb1, wb2), (ca1, ca2), (rp1, rp2), (ic1, ic2)
    olds, cols, rns, cns = (r1, r2), (c1, c2), (rn1, rn2), (cn1, cn2)
    tile = g1.shape[0]
    quarter, half = tile // dp_n, tile // (2 * dp_n)
    widths = (g1.shape[1], g2.shape[1])
    steps = dp_n - 1
    dp, row, col = lax.axis_index("dp"), lax.axis_index("row"), lax.axis_index("col")
    pos = gray(dp)
    plane_n = dp_n * row_n
    slot = pos * row_n + row
    subs = [(m, j) for m in range(2) for j in range(CUTS[m])]

    def plane_peer(i):
        other = (slot + i) % plane_n
        return {"dp": gray(other // row_n), "row": other % row_n}

    def col_peer(i):
        return {"col": (col + i) % col_n}

    def block(d, back):
        return (pos + dp_n - back) % dp_n if d == 0 else (pos + back) % dp_n

    def place(m, j, d, at):
        n = half // CUTS[m]
        return pl.ds(pl.multiple_of(at * quarter + d * half + j * n, 8), n)

    def piece(m, j):
        n = half // CUTS[m]
        return pl.ds(j * n, n)

    def load(d, s, k):
        m, j = subs[k]
        return pltpu.make_async_copy(
            grads[m].at[place(m, j, d, block(d, s + 2)), :],
            lbs[m].at[d, s, piece(m, j), :],
            load_sem.at[d, s, k],
        )

    def keep(d, k):
        m, j = subs[k]
        return pltpu.make_async_copy(
            rbs[m].at[d, steps - 1, piece(m, j), :],
            fulls[m].at[place(m, j, d, pos), :],
            keep_sem.at[d, k],
        )

    def send(d, s, k):
        m, j = subs[k]
        if s < steps:
            if s == 0:
                src = grads[m].at[place(m, j, d, block(d, 1)), :]
            else:
                src = rbs[m].at[d, s - 1, piece(m, j), :]
            dst = rbs[m].at[d, s, piece(m, j), :]
        else:
            t = s - steps
            dst = fulls[m].at[place(m, j, d, block(d, t)), :]
            src = rbs[m].at[d, steps - 1, piece(m, j), :] if t == 0 else dst
        to = gray((pos + 1) % dp_n if d == 0 else (pos + dp_n - 1) % dp_n)
        return pltpu.make_async_remote_copy(
            src_ref=src, dst_ref=dst,
            send_sem=send_sem.at[d, s, k], recv_sem=recv_sem.at[d, s, k],
            device_id={"dp": to}, device_id_type=MESH,
        )

    def message(own, inbox, ss, qs, i, peer):
        return pltpu.make_async_remote_copy(
            src_ref=own, dst_ref=inbox.at[i],
            send_sem=ss.at[i], recv_sem=qs.at[i],
            device_id=peer(i), device_id_type=MESH,
        )

    def exchange(own, inbox, ss, qs, n, peer):
        for i in range(1, n):
            message(own, inbox, ss, qs, i, peer).start()

    def arrive(own, inbox, ss, qs, n, peer):
        for i in range(1, n):
            message(own, inbox, ss, qs, i, peer).wait()

    barrier = pltpu.get_barrier_semaphore()
    for i in range(1, plane_n):
        pl.semaphore_signal(barrier, inc=1, device_id=plane_peer(i), device_id_type=MESH)
    for i in range(1, col_n):
        pl.semaphore_signal(barrier, inc=1, device_id=col_peer(i), device_id_type=MESH)
    pl.semaphore_wait(barrier, plane_n + col_n - 2)

    ks = range(len(subs))
    for k in ks:
        for d in range(2):
            send(d, 0, k).start()
    for s in range(steps):
        for k in ks:
            for d in range(2):
                load(d, s, k).start()
        if s == 0:
            w_loads = []
            for m in range(2):
                w_loads.append(
                    pltpu.make_async_copy(
                        wts[m].at[pl.ds(pl.multiple_of(pos * quarter, 16), quarter), :],
                        wbs[m], w_sem.at[m],
                    )
                )
                w_loads[m].start()
    for m in range(2):
        cas[m][...] = jnp.zeros_like(cas[m])
        w_loads[m].wait()
        n_strip = 16

        def weight_strip(i, acc, m=m):
            x = wbs[m][pl.ds(pl.multiple_of(i * n_strip, n_strip), n_strip), :].astype(jnp.float32)
            return acc + lane_sums(x * x)

        acc = lax.fori_loop(0, quarter // n_strip, weight_strip, jnp.zeros((n_strip, LANES), jnp.float32))
        at = (2 + m) * LANES
        own_upd[:, at : at + LANES] = jnp.sum(acc, axis=0, keepdims=True)

    for s in range(steps):
        for k in ks:
            m, j = subs[k]
            n = half // CUTS[m]
            for d in range(2):
                send(d, s, k).wait_recv()
                load(d, s, k).wait()

                def add_strip(i, carry, m=m, j=j, d=d, s=s, n=n):
                    at = pl.multiple_of(j * n + i * STRIP, STRIP)
                    x = rbs[m][d, s, pl.ds(at, STRIP), :] + lbs[m][d, s, pl.ds(at, STRIP), :]
                    rbs[m][d, s, pl.ds(at, STRIP), :] = x
                    if s == steps - 1:
                        square = x * x + 1e-30
                        rps[m][pl.ds(pl.multiple_of(d * half + at, STRIP), STRIP), :] = lane_sums(square)
                        cas[m][...] += square
                    return carry

                lax.fori_loop(0, n // STRIP, add_strip, 0)
                send(d, s + 1, k).start()
                if s == steps - 1:
                    keep(d, k).start()

    for m in range(2):
        to_lanes(rps[m], own_row, m * quarter)
        at = m * widths[0]
        own_col[:, at : at + widths[m]] = jnp.sum(cas[m][...], axis=0, keepdims=True)
    exchange(own_row, row_msg, s_row, q_row, col_n, col_peer)
    exchange(own_col, col_msg, s_col, q_col, plane_n, plane_peer)

    def forward(t):
        for k in ks:
            for d in range(2):
                send(d, steps + t, k).wait_recv()
                if t < steps - 1:
                    send(d, steps + t + 1, k).start()

    forward(0)
    arrive(own_row, row_msg, s_row, q_row, col_n, col_peer)
    arrive(own_col, col_msg, s_col, q_col, plane_n, plane_peer)
    decay = decay_ref[0]
    rest = 1.0 - decay
    row_tot, col_tot = own_row[...], own_col[...]
    for i in range(1, col_n):
        row_tot = row_tot + row_msg[i]
    for i in range(1, plane_n):
        col_tot = col_tot + col_msg[i]
    for m in range(2):
        row_new = decay * olds[m][pos] + rest * (
            row_tot[:, m * quarter : (m + 1) * quarter] / (widths[m] * col_n)
        )
        at = m * widths[0]
        col_new = decay * cols[m][...] + rest * (col_tot[:, at : at + widths[m]] / (tile * row_n))
        own_end[:, m * quarter : (m + 1) * quarter] = row_new
        cns[m][...] = col_new
        ics[m][...] = jnp.broadcast_to(1.0 / col_new, ics[m].shape)
        for d in range(2):

            def update_strip(i, carry, m=m, d=d):
                at = pl.multiple_of(i * STRIP, STRIP)
                x = rbs[m][d, steps - 1, pl.ds(at, STRIP), :]
                rps[m][pl.ds(pl.multiple_of(d * half + at, STRIP), STRIP), :] = lane_sums(x * x * ics[m][...])
                return carry

            lax.fori_loop(0, half // STRIP, update_strip, 0)
        to_lanes(rps[m], own_row, m * quarter)
        ratio = own_row[:, m * quarter : (m + 1) * quarter] / row_new
        own_upd[:, m * LANES : (m + 1) * LANES] = lane_sums(ratio)
    exchange(own_upd, upd_msg, s_upd, q_upd, col_n, col_peer)
    forward(1)
    arrive(own_upd, upd_msg, s_upd, q_upd, col_n, col_peer)
    upd = own_upd[...]
    for i in range(1, col_n):
        upd = upd + upd_msg[i]
    own_end[:, 2 * quarter :] = upd
    exchange(own_end, end_msg, s_end, q_end, plane_n, plane_peer)
    for t in range(2, steps):
        forward(t)
    arrive(own_end, end_msg, s_end, q_end, plane_n, plane_peer)
    end = own_end[...]
    for i in range(1, plane_n):
        end = end + end_msg[i]
    tot[...] = end
    for m in range(2):
        rns[m][pos] = own_end[:, m * quarter : (m + 1) * quarter]
        for b in range(1, dp_n):
            rns[m][(pos + dp_n - b) % dp_n] = end_msg[b * row_n, :, m * quarter : (m + 1) * quarter]
    for k in ks:
        for d in range(2):
            keep(d, k).wait()
            for s in range(2 * steps):
                send(d, s, k).wait_send()


def gather_sum(sizes, decay, grads, weights, rows, cols):
    dp_n, row_n, col_n = sizes
    tile = grads[0].shape[0]
    widths = tuple(g.shape[1] for g in grads)
    quarter, half = tile // dp_n, tile // (2 * dp_n)
    plane_n, steps, pieces = dp_n * row_n, dp_n - 1, sum(CUTS)
    f32 = jnp.float32
    shape = jax.ShapeDtypeStruct
    hbm = pl.BlockSpec(memory_space=pltpu.HBM)
    vmem = pl.BlockSpec(memory_space=pltpu.VMEM)
    smem = pl.BlockSpec(memory_space=pltpu.SMEM)
    dma = pltpu.SemaphoreType.DMA
    n_end = 2 * quarter + 4 * LANES
    scratch = [pltpu.VMEM((2, steps, half, n), f32) for n in widths] * 2
    scratch += [pltpu.VMEM((quarter, n), jnp.bfloat16) for n in widths]
    scratch += [pltpu.VMEM((STRIP, n), f32) for n in widths]
    scratch += [pltpu.VMEM((quarter, LANES), f32) for n in widths]
    scratch += [pltpu.VMEM((STRIP, n), f32) for n in widths]
    boxes = ((col_n, 2 * quarter), (plane_n, sum(widths)), (col_n, 4 * LANES), (plane_n, n_end))
    scratch += [pltpu.VMEM((n, 1, size), f32) for n, size in boxes]
    scratch += [pltpu.VMEM((1, size), f32) for n, size in boxes]
    scratch += [dma((2, 2 * steps, pieces)), dma((2, 2 * steps, pieces))]
    scratch += [dma((2, steps, pieces)), dma((2, pieces)), dma((2,))]
    for n, size in boxes:
        scratch += [dma((n,)), dma((n,))]
    return pl.pallas_call(
        functools.partial(kernel, sizes),
        out_shape=[shape((tile, n), f32) for n in widths]
        + [shape((dp_n, 1, quarter), f32)] * 2
        + [shape((1, n), f32) for n in widths]
        + [shape((1, n_end), f32)],
        in_specs=[smem] + [hbm] * 4 + [vmem] * 4,
        out_specs=[hbm] * 2 + [vmem] * 5,
        scratch_shapes=scratch,
        compiler_params=pltpu.CompilerParams(
            collective_id=0, has_side_effects=True, vmem_limit_bytes=58 * 2**20
        ),
    )(
        decay, *grads, *weights,
        *(r.reshape(dp_n, 1, quarter) for r in rows),
        *(c.reshape(1, -1) for c in cols),
    )


def body(
    sizes,
    step_count,
    ffn_weight, ffn_grads, ffn_rows, ffn_cols,
    attn_weight, attn_grads, attn_rows, attn_cols,
):
    dp_n, row_n, col_n = sizes
    decay = 1.0 - step_count.astype(jnp.float32) ** (-0.8)
    weights = (ffn_weight, attn_weight)
    full1, full2, rn1, rn2, cn1, cn2, tot = gather_sum(
        sizes, decay, (ffn_grads[0], attn_grads[0]), weights,
        (ffn_rows, attn_rows), (ffn_cols, attn_cols),
    )
    quarter = ffn_weight.shape[0] // dp_n
    tot = tot[0]
    outs = []
    for m, (full, rn, cn) in enumerate(((full1, rn1, cn1), (full2, rn2, cn2))):
        high = weights[m].shape[0] * row_n
        wide = weights[m].shape[1] * col_n
        entries = high * wide
        mean = jnp.sum(tot[m * quarter : (m + 1) * quarter]) / high
        at = 2 * quarter + m * LANES
        update_rms = jnp.sqrt(mean * jnp.sum(tot[at : at + LANES]) / entries)
        at += 2 * LANES
        factor = 0.01 * jnp.sqrt(jnp.sum(tot[at : at + LANES]) / entries)
        rows_new, cols_new = rn.reshape(-1), cn.reshape(-1)
        second = rows_new[:, None] * cols_new[None, :] / mean
        update = full / jnp.sqrt(second) / jnp.maximum(1.0, update_rms)
        fresh = weights[m].astype(jnp.float32) - factor * update
        outs += [fresh, update, rows_new, cols_new]
    return tuple(outs)


def solution(mesh):
    sizes = (mesh.shape["dp"], mesh.shape["row"], mesh.shape["col"])
    tiles = P("row", "col")
    grads = P("dp", "row", "col")
    one = (tiles, grads, P("row"), P("col"))
    result = (tiles, tiles, P("row"), P("col"))
    return jax.shard_map(
        functools.partial(body, sizes),
        mesh=mesh,
        in_specs=(P(), *one, *one),
        out_specs=(*result, *result),
        check_vma=False,
    )
```

```python
import functools

import jax
import jax.numpy as jnp
from jax import lax
from jax.experimental import pallas as pl
from jax.experimental.pallas import tpu as pltpu
from jax.sharding import PartitionSpec as P

MESH = pl.DeviceIdType.MESH
LANES = 128
STRIP = 8
CUTS = (4, 2)
LATE = 1


def gray(index):
    high = index // 2
    return index + high * (5 - 2 * index)


def lane_sums(x):
    total = x[:, :LANES]
    for c in range(1, x.shape[1] // LANES):
        total = total + x[:, c * LANES : (c + 1) * LANES]
    return total


def to_lanes(ref, out_ref, at):
    rows = ref.shape[0]
    for c in range(rows // LANES):
        turned = ref[pl.ds(c * LANES, LANES), :].T
        out_ref[:, pl.ds(at + c * LANES, LANES)] = jnp.sum(turned, axis=0, keepdims=True)


def kernel(
    sizes,
    decay_ref,
    g1, g2, w1, w2, r1, r2, c1, c2,
    full1, full2, rn1, rn2, cn1, cn2, tot,
    rb1, rb2, lb1, lb2, wb1, wb2, ca1, ca2, rp1, rp2, ic1, ic2,
    row_msg, col_msg, upd_msg, end_msg,
    own_row, own_col, own_upd, own_end,
    send_sem, recv_sem, load_sem, keep_sem, w_sem,
    s_row, q_row, s_col, q_col, s_upd, q_upd, s_end, q_end,
):
    dp_n, row_n, col_n = sizes
    grads, fulls, rbs, lbs = (g1, g2), (full1, full2), (rb1, rb2), (lb1, lb2)
    wts, wbs, cas, rps, ics = (w1, w2), (wb1, wb2), (ca1, ca2), (rp1, rp2), (ic1, ic2)
    olds, cols, rns, cns = (r1, r2), (c1, c2), (rn1, rn2), (cn1, cn2)
    tile = g1.shape[0]
    quarter, half = tile // dp_n, tile // (2 * dp_n)
    widths = (g1.shape[1], g2.shape[1])
    steps = dp_n - 1
    dp, row, col = lax.axis_index("dp"), lax.axis_index("row"), lax.axis_index("col")
    pos = gray(dp)
    plane_n = dp_n * row_n
    slot = pos * row_n + row
    subs = [(m, j) for m in range(2) for j in range(CUTS[m])]

    def hops(k):
        return 2 * steps - (subs[k][0] == LATE)

    def plane_peer(i):
        other = (slot + i) % plane_n
        return {"dp": gray(other // row_n), "row": other % row_n}

    def col_peer(i):
        return {"col": (col + i) % col_n}

    def block(d, back):
        return (pos + dp_n - back) % dp_n if d == 0 else (pos + back) % dp_n

    def place(m, j, d, at):
        n = half // CUTS[m]
        return pl.ds(pl.multiple_of(at * quarter + d * half + j * n, 8), n)

    def piece(m, j):
        n = half // CUTS[m]
        return pl.ds(j * n, n)

    def load(d, s, k):
        m, j = subs[k]
        return pltpu.make_async_copy(
            grads[m].at[place(m, j, d, block(d, s + 2)), :],
            lbs[m].at[d, s, piece(m, j), :],
            load_sem.at[d, s, k],
        )

    def keep(d, k):
        m, j = subs[k]
        return pltpu.make_async_copy(
            rbs[m].at[d, steps - 1, piece(m, j), :],
            fulls[m].at[place(m, j, d, pos), :],
            keep_sem.at[d, k],
        )

    def send(d, s, k):
        m, j = subs[k]
        if s < steps:
            if s == 0:
                src = grads[m].at[place(m, j, d, block(d, 1)), :]
            else:
                src = rbs[m].at[d, s - 1, piece(m, j), :]
            dst = rbs[m].at[d, s, piece(m, j), :]
        else:
            t = s - steps
            dst = fulls[m].at[place(m, j, d, block(d, t)), :]
            src = rbs[m].at[d, steps - 1, piece(m, j), :] if t == 0 else dst
        to = gray((pos + 1) % dp_n if d == 0 else (pos + dp_n - 1) % dp_n)
        return pltpu.make_async_remote_copy(
            src_ref=src, dst_ref=dst,
            send_sem=send_sem.at[d, s, k], recv_sem=recv_sem.at[d, s, k],
            device_id={"dp": to}, device_id_type=MESH,
        )

    def message(own, inbox, ss, qs, i, peer):
        return pltpu.make_async_remote_copy(
            src_ref=own, dst_ref=inbox.at[i],
            send_sem=ss.at[i], recv_sem=qs.at[i],
            device_id=peer(i), device_id_type=MESH,
        )

    def exchange(own, inbox, ss, qs, n, peer):
        for i in range(1, n):
            message(own, inbox, ss, qs, i, peer).start()

    def arrive(own, inbox, ss, qs, n, peer):
        for i in range(1, n):
            message(own, inbox, ss, qs, i, peer).wait()

    barrier = pltpu.get_barrier_semaphore()
    for i in range(1, plane_n):
        pl.semaphore_signal(barrier, inc=1, device_id=plane_peer(i), device_id_type=MESH)
    for i in range(1, col_n):
        pl.semaphore_signal(barrier, inc=1, device_id=col_peer(i), device_id_type=MESH)
    pl.semaphore_wait(barrier, plane_n + col_n - 2)

    ks = range(len(subs))
    for k in ks:
        for d in range(2):
            send(d, 0, k).start()
    for s in range(steps):
        for k in ks:
            for d in range(2):
                load(d, s, k).start()
        if s == 0:
            w_loads = []
            for m in range(2):
                w_loads.append(
                    pltpu.make_async_copy(
                        wts[m].at[pl.ds(pl.multiple_of(pos * quarter, 16), quarter), :],
                        wbs[m], w_sem.at[m],
                    )
                )
                w_loads[m].start()
    for m in range(2):
        cas[m][...] = jnp.zeros_like(cas[m])
        w_loads[m].wait()
        n_strip = 16

        def weight_strip(i, acc, m=m):
            x = wbs[m][pl.ds(pl.multiple_of(i * n_strip, n_strip), n_strip), :].astype(jnp.float32)
            return acc + lane_sums(x * x)

        acc = lax.fori_loop(0, quarter // n_strip, weight_strip, jnp.zeros((n_strip, LANES), jnp.float32))
        at = (2 + m) * LANES
        own_upd[:, at : at + LANES] = jnp.sum(acc, axis=0, keepdims=True)

    for s in range(steps):
        for k in ks:
            m, j = subs[k]
            n = half // CUTS[m]
            for d in range(2):
                send(d, s, k).wait_recv()
                load(d, s, k).wait()

                def add_strip(i, carry, m=m, j=j, d=d, s=s, n=n):
                    at = pl.multiple_of(j * n + i * STRIP, STRIP)
                    x = rbs[m][d, s, pl.ds(at, STRIP), :] + lbs[m][d, s, pl.ds(at, STRIP), :]
                    rbs[m][d, s, pl.ds(at, STRIP), :] = x
                    if s == steps - 1:
                        square = x * x + 1e-30
                        rps[m][pl.ds(pl.multiple_of(d * half + at, STRIP), STRIP), :] = lane_sums(square)
                        cas[m][...] += square
                    return carry

                lax.fori_loop(0, n // STRIP, add_strip, 0)
                send(d, s + 1, k).start()
                if s == steps - 1:
                    keep(d, k).start()

    for m in range(2):
        to_lanes(rps[m], own_row, m * quarter)
        at = m * widths[0]
        own_col[:, at : at + widths[m]] = jnp.sum(cas[m][...], axis=0, keepdims=True)
    exchange(own_row, row_msg, s_row, q_row, col_n, col_peer)
    exchange(own_col, col_msg, s_col, q_col, plane_n, plane_peer)

    def forward(t):
        for k in ks:
            for d in range(2):
                if t < hops(k) - steps:
                    send(d, steps + t, k).wait_recv()
                if t + 1 < hops(k) - steps:
                    send(d, steps + t + 1, k).start()

    forward(0)
    arrive(own_row, row_msg, s_row, q_row, col_n, col_peer)
    arrive(own_col, col_msg, s_col, q_col, plane_n, plane_peer)
    decay = decay_ref[0]
    rest = 1.0 - decay
    row_tot, col_tot = own_row[...], own_col[...]
    for i in range(1, col_n):
        row_tot = row_tot + row_msg[i]
    for i in range(1, plane_n):
        col_tot = col_tot + col_msg[i]
    for m in range(2):
        row_new = decay * olds[m][pos] + rest * (
            row_tot[:, m * quarter : (m + 1) * quarter] / (widths[m] * col_n)
        )
        at = m * widths[0]
        col_new = decay * cols[m][...] + rest * (col_tot[:, at : at + widths[m]] / (tile * row_n))
        own_end[:, m * quarter : (m + 1) * quarter] = row_new
        cns[m][...] = col_new
        ics[m][...] = jnp.broadcast_to(1.0 / col_new, ics[m].shape)
        for d in range(2):

            def update_strip(i, carry, m=m, d=d):
                at = pl.multiple_of(i * STRIP, STRIP)
                x = rbs[m][d, steps - 1, pl.ds(at, STRIP), :]
                rps[m][pl.ds(pl.multiple_of(d * half + at, STRIP), STRIP), :] = lane_sums(x * x * ics[m][...])
                return carry

            lax.fori_loop(0, half // STRIP, update_strip, 0)
        to_lanes(rps[m], own_row, m * quarter)
        ratio = own_row[:, m * quarter : (m + 1) * quarter] / row_new
        own_upd[:, m * LANES : (m + 1) * LANES] = lane_sums(ratio)
    exchange(own_upd, upd_msg, s_upd, q_upd, col_n, col_peer)
    forward(1)
    arrive(own_upd, upd_msg, s_upd, q_upd, col_n, col_peer)
    upd = own_upd[...]
    for i in range(1, col_n):
        upd = upd + upd_msg[i]
    own_end[:, 2 * quarter :] = upd
    exchange(own_end, end_msg, s_end, q_end, plane_n, plane_peer)
    for t in range(2, steps):
        forward(t)
    arrive(own_end, end_msg, s_end, q_end, plane_n, plane_peer)
    end = own_end[...]
    for i in range(1, plane_n):
        end = end + end_msg[i]
    tot[...] = end
    for m in range(2):
        rns[m][pos] = own_end[:, m * quarter : (m + 1) * quarter]
        for b in range(1, dp_n):
            rns[m][(pos + dp_n - b) % dp_n] = end_msg[b * row_n, :, m * quarter : (m + 1) * quarter]
    for k in ks:
        for d in range(2):
            keep(d, k).wait()
            for s in range(hops(k)):
                send(d, s, k).wait_send()


def gather_sum(sizes, decay, grads, weights, rows, cols):
    dp_n, row_n, col_n = sizes
    tile = grads[0].shape[0]
    widths = tuple(g.shape[1] for g in grads)
    quarter, half = tile // dp_n, tile // (2 * dp_n)
    plane_n, steps, pieces = dp_n * row_n, dp_n - 1, sum(CUTS)
    f32 = jnp.float32
    shape = jax.ShapeDtypeStruct
    hbm = pl.BlockSpec(memory_space=pltpu.HBM)
    vmem = pl.BlockSpec(memory_space=pltpu.VMEM)
    smem = pl.BlockSpec(memory_space=pltpu.SMEM)
    dma = pltpu.SemaphoreType.DMA
    n_end = 2 * quarter + 4 * LANES
    scratch = [pltpu.VMEM((2, steps, half, n), f32) for n in widths] * 2
    scratch += [pltpu.VMEM((quarter, n), jnp.bfloat16) for n in widths]
    scratch += [pltpu.VMEM((STRIP, n), f32) for n in widths]
    scratch += [pltpu.VMEM((quarter, LANES), f32) for n in widths]
    scratch += [pltpu.VMEM((STRIP, n), f32) for n in widths]
    boxes = ((col_n, 2 * quarter), (plane_n, sum(widths)), (col_n, 4 * LANES), (plane_n, n_end))
    scratch += [pltpu.VMEM((n, 1, size), f32) for n, size in boxes]
    scratch += [pltpu.VMEM((1, size), f32) for n, size in boxes]
    scratch += [dma((2, 2 * steps, pieces)), dma((2, 2 * steps, pieces))]
    scratch += [dma((2, steps, pieces)), dma((2, pieces)), dma((2,))]
    for n, size in boxes:
        scratch += [dma((n,)), dma((n,))]
    return pl.pallas_call(
        functools.partial(kernel, sizes),
        out_shape=[shape((tile, n), f32) for n in widths]
        + [shape((dp_n, 1, quarter), f32)] * 2
        + [shape((1, n), f32) for n in widths]
        + [shape((1, n_end), f32)],
        in_specs=[smem] + [hbm] * 4 + [vmem] * 4,
        out_specs=[hbm] * 2 + [vmem] * 5,
        scratch_shapes=scratch,
        compiler_params=pltpu.CompilerParams(
            collective_id=0, has_side_effects=True, vmem_limit_bytes=58 * 2**20
        ),
    )(
        decay, *grads, *weights,
        *(r.reshape(dp_n, 1, quarter) for r in rows),
        *(c.reshape(1, -1) for c in cols),
    )


def last_hop(full, dp_n):
    pos = gray(lax.axis_index("dp"))
    quarter, half = full.shape[0] // dp_n, full.shape[0] // (2 * dp_n)
    ring = [gray(p) for p in range(dp_n)]
    turns = ((0, 1), (1, dp_n - 1))
    sent = []
    for d, turn in turns:
        at = (pos + turn * 2) % dp_n * quarter + d * half
        sent.append(lax.dynamic_slice_in_dim(full, at, half, 0))
    full, *sent = lax.optimization_barrier((full, *sent))
    came = []
    for d, turn in turns:
        pairs = [(ring[p], ring[(p + turn) % dp_n]) for p in range(dp_n)]
        came.append(lax.ppermute(sent[d], "dp", pairs))
    for d, turn in turns:
        at = (pos + turn) % dp_n * quarter + d * half
        full = lax.dynamic_update_slice_in_dim(full, came[d], at, 0)
    return full


def body(
    sizes,
    step_count,
    ffn_weight, ffn_grads, ffn_rows, ffn_cols,
    attn_weight, attn_grads, attn_rows, attn_cols,
):
    dp_n, row_n, col_n = sizes
    decay = 1.0 - step_count.astype(jnp.float32) ** (-0.8)
    weights = (ffn_weight, attn_weight)
    full1, full2, rn1, rn2, cn1, cn2, tot = gather_sum(
        sizes, decay, (ffn_grads[0], attn_grads[0]), weights,
        (ffn_rows, attn_rows), (ffn_cols, attn_cols),
    )
    full2 = last_hop(full2, dp_n)
    quarter = ffn_weight.shape[0] // dp_n
    tot = tot[0]
    outs = []
    for m, (full, rn, cn) in enumerate(((full1, rn1, cn1), (full2, rn2, cn2))):
        high = weights[m].shape[0] * row_n
        wide = weights[m].shape[1] * col_n
        entries = high * wide
        mean = jnp.sum(tot[m * quarter : (m + 1) * quarter]) / high
        at = 2 * quarter + m * LANES
        update_rms = jnp.sqrt(mean * jnp.sum(tot[at : at + LANES]) / entries)
        at += 2 * LANES
        factor = 0.01 * jnp.sqrt(jnp.sum(tot[at : at + LANES]) / entries)
        rows_new, cols_new = rn.reshape(-1), cn.reshape(-1)
        second = rows_new[:, None] * cols_new[None, :] / mean
        update = full / jnp.sqrt(second) / jnp.maximum(1.0, update_rms)
        fresh = weights[m].astype(jnp.float32) - factor * update
        outs += [fresh, update, rows_new, cols_new]
    return tuple(outs)


def solution(mesh):
    sizes = (mesh.shape["dp"], mesh.shape["row"], mesh.shape["col"])
    tiles = P("row", "col")
    grads = P("dp", "row", "col")
    one = (tiles, grads, P("row"), P("col"))
    result = (tiles, tiles, P("row"), P("col"))
    return jax.shard_map(
        functools.partial(body, sizes),
        mesh=mesh,
        in_specs=(P(), *one, *one),
        out_specs=(*result, *result),
        check_vma=False,
    )
```

```python
import functools

import jax
import jax.numpy as jnp
from jax import lax
from jax.experimental import pallas as pl
from jax.experimental.pallas import tpu as pltpu
from jax.sharding import PartitionSpec as P

MESH = pl.DeviceIdType.MESH
LANES = 128
STRIP = 8
CUTS = (4, 2)
LATE = 1


def gray(index):
    high = index // 2
    return index + high * (5 - 2 * index)


def lane_sums(x):
    total = x[:, :LANES]
    for c in range(1, x.shape[1] // LANES):
        total = total + x[:, c * LANES : (c + 1) * LANES]
    return total


def to_lanes(ref, out_ref, at):
    rows = ref.shape[0]
    for c in range(rows // LANES):
        turned = ref[pl.ds(c * LANES, LANES), :].T
        out_ref[:, pl.ds(at + c * LANES, LANES)] = jnp.sum(turned, axis=0, keepdims=True)


def kernel(
    sizes,
    decay_ref,
    g1, g2, w1, w2, r1, r2, c1, c2,
    full1, full2, rn1, rn2, cn1, cn2, tot, late1, late2,
    rb1, rb2, lb1, lb2, wb1, wb2, ca1, ca2, rp1, rp2, ic1, ic2,
    row_msg, col_msg, upd_msg, end_msg,
    own_row, own_col, own_upd, own_end,
    send_sem, recv_sem, load_sem, keep_sem, w_sem, late_sem,
    s_row, q_row, s_col, q_col, s_upd, q_upd, s_end, q_end,
):
    dp_n, row_n, col_n = sizes
    grads, fulls, rbs, lbs = (g1, g2), (full1, full2), (rb1, rb2), (lb1, lb2)
    wts, wbs, cas, rps, ics = (w1, w2), (wb1, wb2), (ca1, ca2), (rp1, rp2), (ic1, ic2)
    olds, cols, rns, cns = (r1, r2), (c1, c2), (rn1, rn2), (cn1, cn2)
    tile = g1.shape[0]
    quarter, half = tile // dp_n, tile // (2 * dp_n)
    widths = (g1.shape[1], g2.shape[1])
    steps = dp_n - 1
    dp, row, col = lax.axis_index("dp"), lax.axis_index("row"), lax.axis_index("col")
    pos = gray(dp)
    plane_n = dp_n * row_n
    slot = pos * row_n + row
    subs = [(m, j) for m in range(2) for j in range(CUTS[m])]

    def hops(k):
        return 2 * steps - (subs[k][0] == LATE)

    def plane_peer(i):
        other = (slot + i) % plane_n
        return {"dp": gray(other // row_n), "row": other % row_n}

    def col_peer(i):
        return {"col": (col + i) % col_n}

    def block(d, back):
        return (pos + dp_n - back) % dp_n if d == 0 else (pos + back) % dp_n

    def place(m, j, d, at):
        n = half // CUTS[m]
        return pl.ds(pl.multiple_of(at * quarter + d * half + j * n, 8), n)

    def piece(m, j):
        n = half // CUTS[m]
        return pl.ds(j * n, n)

    def load(d, s, k):
        m, j = subs[k]
        return pltpu.make_async_copy(
            grads[m].at[place(m, j, d, block(d, s + 2)), :],
            lbs[m].at[d, s, piece(m, j), :],
            load_sem.at[d, s, k],
        )

    def keep(d, k):
        m, j = subs[k]
        return pltpu.make_async_copy(
            rbs[m].at[d, steps - 1, piece(m, j), :],
            fulls[m].at[place(m, j, d, pos), :],
            keep_sem.at[d, k],
        )

    def set_aside(d, k):
        m, j = subs[k]
        return pltpu.make_async_copy(
            fulls[m].at[place(m, j, d, block(d, steps - 1)), :],
            (late1, late2)[d].at[piece(m, j), :],
            late_sem.at[d, k],
        )

    def send(d, s, k):
        m, j = subs[k]
        if s < steps:
            if s == 0:
                src = grads[m].at[place(m, j, d, block(d, 1)), :]
            else:
                src = rbs[m].at[d, s - 1, piece(m, j), :]
            dst = rbs[m].at[d, s, piece(m, j), :]
        else:
            t = s - steps
            dst = fulls[m].at[place(m, j, d, block(d, t)), :]
            src = rbs[m].at[d, steps - 1, piece(m, j), :] if t == 0 else dst
        to = gray((pos + 1) % dp_n if d == 0 else (pos + dp_n - 1) % dp_n)
        return pltpu.make_async_remote_copy(
            src_ref=src, dst_ref=dst,
            send_sem=send_sem.at[d, s, k], recv_sem=recv_sem.at[d, s, k],
            device_id={"dp": to}, device_id_type=MESH,
        )

    def message(own, inbox, ss, qs, i, peer):
        return pltpu.make_async_remote_copy(
            src_ref=own, dst_ref=inbox.at[i],
            send_sem=ss.at[i], recv_sem=qs.at[i],
            device_id=peer(i), device_id_type=MESH,
        )

    def exchange(own, inbox, ss, qs, n, peer):
        for i in range(1, n):
            message(own, inbox, ss, qs, i, peer).start()

    def arrive(own, inbox, ss, qs, n, peer):
        for i in range(1, n):
            message(own, inbox, ss, qs, i, peer).wait()

    barrier = pltpu.get_barrier_semaphore()
    for i in range(1, plane_n):
        pl.semaphore_signal(barrier, inc=1, device_id=plane_peer(i), device_id_type=MESH)
    for i in range(1, col_n):
        pl.semaphore_signal(barrier, inc=1, device_id=col_peer(i), device_id_type=MESH)
    pl.semaphore_wait(barrier, plane_n + col_n - 2)

    ks = range(len(subs))
    for k in ks:
        for d in range(2):
            send(d, 0, k).start()
    for s in range(steps):
        for k in ks:
            for d in range(2):
                load(d, s, k).start()
        if s == 0:
            w_loads = []
            for m in range(2):
                w_loads.append(
                    pltpu.make_async_copy(
                        wts[m].at[pl.ds(pl.multiple_of(pos * quarter, 16), quarter), :],
                        wbs[m], w_sem.at[m],
                    )
                )
                w_loads[m].start()
    for m in range(2):
        cas[m][...] = jnp.zeros_like(cas[m])
        w_loads[m].wait()
        n_strip = 16

        def weight_strip(i, acc, m=m):
            x = wbs[m][pl.ds(pl.multiple_of(i * n_strip, n_strip), n_strip), :].astype(jnp.float32)
            return acc + lane_sums(x * x)

        acc = lax.fori_loop(0, quarter // n_strip, weight_strip, jnp.zeros((n_strip, LANES), jnp.float32))
        at = (2 + m) * LANES
        own_upd[:, at : at + LANES] = jnp.sum(acc, axis=0, keepdims=True)

    for s in range(steps):
        for k in ks:
            m, j = subs[k]
            n = half // CUTS[m]
            for d in range(2):
                send(d, s, k).wait_recv()
                load(d, s, k).wait()

                def add_strip(i, carry, m=m, j=j, d=d, s=s, n=n):
                    at = pl.multiple_of(j * n + i * STRIP, STRIP)
                    x = rbs[m][d, s, pl.ds(at, STRIP), :] + lbs[m][d, s, pl.ds(at, STRIP), :]
                    rbs[m][d, s, pl.ds(at, STRIP), :] = x
                    if s == steps - 1:
                        square = x * x + 1e-30
                        rps[m][pl.ds(pl.multiple_of(d * half + at, STRIP), STRIP), :] = lane_sums(square)
                        cas[m][...] += square
                    return carry

                lax.fori_loop(0, n // STRIP, add_strip, 0)
                send(d, s + 1, k).start()
                if s == steps - 1:
                    keep(d, k).start()

    for m in range(2):
        to_lanes(rps[m], own_row, m * quarter)
        at = m * widths[0]
        own_col[:, at : at + widths[m]] = jnp.sum(cas[m][...], axis=0, keepdims=True)
    exchange(own_row, row_msg, s_row, q_row, col_n, col_peer)
    exchange(own_col, col_msg, s_col, q_col, plane_n, plane_peer)

    def forward(t):
        for k in ks:
            for d in range(2):
                if t < hops(k) - steps:
                    send(d, steps + t, k).wait_recv()
                if t + 1 < hops(k) - steps:
                    send(d, steps + t + 1, k).start()
                if subs[k][0] == LATE and t == steps - 2:
                    set_aside(d, k).start()

    forward(0)
    arrive(own_row, row_msg, s_row, q_row, col_n, col_peer)
    arrive(own_col, col_msg, s_col, q_col, plane_n, plane_peer)
    decay = decay_ref[0]
    rest = 1.0 - decay
    row_tot, col_tot = own_row[...], own_col[...]
    for i in range(1, col_n):
        row_tot = row_tot + row_msg[i]
    for i in range(1, plane_n):
        col_tot = col_tot + col_msg[i]
    for m in range(2):
        row_new = decay * olds[m][pos] + rest * (
            row_tot[:, m * quarter : (m + 1) * quarter] / (widths[m] * col_n)
        )
        at = m * widths[0]
        col_new = decay * cols[m][...] + rest * (col_tot[:, at : at + widths[m]] / (tile * row_n))
        own_end[:, m * quarter : (m + 1) * quarter] = row_new
        cns[m][...] = col_new
        ics[m][...] = jnp.broadcast_to(1.0 / col_new, ics[m].shape)
        for d in range(2):

            def update_strip(i, carry, m=m, d=d):
                at = pl.multiple_of(i * STRIP, STRIP)
                x = rbs[m][d, steps - 1, pl.ds(at, STRIP), :]
                rps[m][pl.ds(pl.multiple_of(d * half + at, STRIP), STRIP), :] = lane_sums(x * x * ics[m][...])
                return carry

            lax.fori_loop(0, half // STRIP, update_strip, 0)
        to_lanes(rps[m], own_row, m * quarter)
        ratio = own_row[:, m * quarter : (m + 1) * quarter] / row_new
        own_upd[:, m * LANES : (m + 1) * LANES] = lane_sums(ratio)
    exchange(own_upd, upd_msg, s_upd, q_upd, col_n, col_peer)
    arrive(own_upd, upd_msg, s_upd, q_upd, col_n, col_peer)
    upd = own_upd[...]
    for i in range(1, col_n):
        upd = upd + upd_msg[i]
    own_end[:, 2 * quarter :] = upd
    exchange(own_end, end_msg, s_end, q_end, plane_n, plane_peer)
    for t in range(1, steps):
        forward(t)
    arrive(own_end, end_msg, s_end, q_end, plane_n, plane_peer)
    end = own_end[...]
    for i in range(1, plane_n):
        end = end + end_msg[i]
    tot[...] = end
    for m in range(2):
        rns[m][pos] = own_end[:, m * quarter : (m + 1) * quarter]
        for b in range(1, dp_n):
            rns[m][(pos + dp_n - b) % dp_n] = end_msg[b * row_n, :, m * quarter : (m + 1) * quarter]
    for k in ks:
        for d in range(2):
            keep(d, k).wait()
            if subs[k][0] == LATE:
                set_aside(d, k).wait()
            for s in range(hops(k)):
                send(d, s, k).wait_send()


def gather_sum(sizes, decay, grads, weights, rows, cols):
    dp_n, row_n, col_n = sizes
    tile = grads[0].shape[0]
    widths = tuple(g.shape[1] for g in grads)
    quarter, half = tile // dp_n, tile // (2 * dp_n)
    plane_n, steps, pieces = dp_n * row_n, dp_n - 1, sum(CUTS)
    f32 = jnp.float32
    shape = jax.ShapeDtypeStruct
    hbm = pl.BlockSpec(memory_space=pltpu.HBM)
    vmem = pl.BlockSpec(memory_space=pltpu.VMEM)
    smem = pl.BlockSpec(memory_space=pltpu.SMEM)
    dma = pltpu.SemaphoreType.DMA
    n_end = 2 * quarter + 4 * LANES
    scratch = [pltpu.VMEM((2, steps, half, n), f32) for n in widths] * 2
    scratch += [pltpu.VMEM((quarter, n), jnp.bfloat16) for n in widths]
    scratch += [pltpu.VMEM((STRIP, n), f32) for n in widths]
    scratch += [pltpu.VMEM((quarter, LANES), f32) for n in widths]
    scratch += [pltpu.VMEM((STRIP, n), f32) for n in widths]
    boxes = ((col_n, 2 * quarter), (plane_n, sum(widths)), (col_n, 4 * LANES), (plane_n, n_end))
    scratch += [pltpu.VMEM((n, 1, size), f32) for n, size in boxes]
    scratch += [pltpu.VMEM((1, size), f32) for n, size in boxes]
    scratch += [dma((2, 2 * steps, pieces)), dma((2, 2 * steps, pieces))]
    scratch += [dma((2, steps, pieces)), dma((2, pieces)), dma((2,)), dma((2, pieces))]
    for n, size in boxes:
        scratch += [dma((n,)), dma((n,))]
    return pl.pallas_call(
        functools.partial(kernel, sizes),
        out_shape=[shape((tile, n), f32) for n in widths]
        + [shape((dp_n, 1, quarter), f32)] * 2
        + [shape((1, n), f32) for n in widths]
        + [shape((1, n_end), f32)]
        + [shape((half, widths[LATE]), f32)] * 2,
        in_specs=[smem] + [hbm] * 4 + [vmem] * 4,
        out_specs=[hbm] * 2 + [vmem] * 5 + [hbm] * 2,
        scratch_shapes=scratch,
        compiler_params=pltpu.CompilerParams(
            collective_id=0, has_side_effects=True, vmem_limit_bytes=58 * 2**20
        ),
    )(
        decay, *grads, *weights,
        *(r.reshape(dp_n, 1, quarter) for r in rows),
        *(c.reshape(1, -1) for c in cols),
    )


def last_hop(full, sent, dp_n):
    pos = gray(lax.axis_index("dp"))
    quarter, half = full.shape[0] // dp_n, full.shape[0] // (2 * dp_n)
    ring = [gray(p) for p in range(dp_n)]
    turns = ((0, 1), (1, dp_n - 1))
    came = []
    for d, turn in turns:
        pairs = [(ring[p], ring[(p + turn) % dp_n]) for p in range(dp_n)]
        came.append(lax.ppermute(sent[d], "dp", pairs))
    for d, turn in turns:
        at = (pos + turn) % dp_n * quarter + d * half
        full = lax.dynamic_update_slice_in_dim(full, came[d], at, 0)
    return full


def body(
    sizes,
    step_count,
    ffn_weight, ffn_grads, ffn_rows, ffn_cols,
    attn_weight, attn_grads, attn_rows, attn_cols,
):
    dp_n, row_n, col_n = sizes
    decay = 1.0 - step_count.astype(jnp.float32) ** (-0.8)
    weights = (ffn_weight, attn_weight)
    full1, full2, rn1, rn2, cn1, cn2, tot, *sent = gather_sum(
        sizes, decay, (ffn_grads[0], attn_grads[0]), weights,
        (ffn_rows, attn_rows), (ffn_cols, attn_cols),
    )
    full2 = last_hop(full2, sent, dp_n)
    quarter = ffn_weight.shape[0] // dp_n
    tot = tot[0]
    outs = []
    for m, (full, rn, cn) in enumerate(((full1, rn1, cn1), (full2, rn2, cn2))):
        high = weights[m].shape[0] * row_n
        wide = weights[m].shape[1] * col_n
        entries = high * wide
        mean = jnp.sum(tot[m * quarter : (m + 1) * quarter]) / high
        at = 2 * quarter + m * LANES
        update_rms = jnp.sqrt(mean * jnp.sum(tot[at : at + LANES]) / entries)
        at += 2 * LANES
        factor = 0.01 * jnp.sqrt(jnp.sum(tot[at : at + LANES]) / entries)
        rows_new, cols_new = rn.reshape(-1), cn.reshape(-1)
        second = rows_new[:, None] * cols_new[None, :] / mean
        update = full / jnp.sqrt(second) / jnp.maximum(1.0, update_rms)
        fresh = weights[m].astype(jnp.float32) - factor * update
        outs += [fresh, update, rows_new, cols_new]
    return tuple(outs)


def solution(mesh):
    sizes = (mesh.shape["dp"], mesh.shape["row"], mesh.shape["col"])
    tiles = P("row", "col")
    grads = P("dp", "row", "col")
    one = (tiles, grads, P("row"), P("col"))
    result = (tiles, tiles, P("row"), P("col"))
    return jax.shard_map(
        functools.partial(body, sizes),
        mesh=mesh,
        in_specs=(P(), *one, *one),
        out_specs=(*result, *result),
        check_vma=False,
    )
```
